32 devices in a mesh: parts: 2 (over x), rep: 2 (over core), tp: 8 (over z, y).
Axes of the slice: x: 2, y: 2, z: 4, core: 2. Of those that a mesh axis runs over, the one named last changes fastest.
Arguments:
- hidden: bfloat16 [4096, 28672], P(('parts', 'rep'), 'tp'), parts along dimension 0, may hold values from -6 to 6
- residual: bfloat16 [4096, 4096], P(('parts', 'rep', 'tp')), parts along dimension 0, may hold values from -6 to 6
- down_weight: bfloat16 [28672, 4096], P('tp'), may hold values from -0.03125 to 0.03125
- shrink_pool: bfloat16 [32, 64, 28672], P('rep', None, 'tp'), may hold values from -0.03125 to 0.03125
- expand_pool: bfloat16 [32, 64, 4096], P('rep', None, 'tp'), may hold values from -0.75 to 0.75
- seg_blocks: int32 [12], P('parts'), parts along dimension 0, may hold values from 1 to 8, 16 in all
- tail_rows: int32 [12], P('parts'), parts along dimension 0, may hold values from 1 to 128
- page_slot: int32 [12], P('parts'), parts along dimension 0, may hold values from 0 to 31, as said below
Outputs:
- mixed: bfloat16 [4096, 4096], P(('parts', 'rep', 'tp')), parts along dimension 0
The draws below stay inside these ranges and needn't reach their ends.
There are 2 independent parts, one for each index of `parts`. The reference program is written for one: setup_inputs(seed, part) draws one part's arguments, and reference() takes and returns one part's arrays. A program takes and returns all parts, laid end to end along the dimension named above; an argument that names none is the same for every part. Nothing has to cross between parts.
Inputs may be any that keep to these rules, and one draw needn't show every extreme that they name: `page_slot`: the 6 pages are distinct; both page 0 and page 32 - 1 are among them.
All inputs are finite; a program needn't handle non-finite values.
Results may differ from the reference program's by a relative error of at most 0.01.
Values may be sent and summed in bfloat16 or wider, within the bound.
A program may use at most 192 MiB of HBM per device.

```python
import math
import jax
import jax.numpy as jnp
import numpy as np
from jax import lax

DOWN_WIDTH = 4096
FF = 28672
RANK = 64
BLOCK = 128
TOTAL_ROWS = 2048
BLOCKS = 16
SEGS = 6
SEG_MOST = 8
SLOTS = 32
N_TP = 8


def draw_page_slot(key, part):
    key = jax.random.fold_in(key, 7)
    first_key, second_key = jax.random.split(key)
    inner = jax.random.permutation(first_key, SLOTS - 2)[:SEGS - 2] + 1
    chosen = jnp.concatenate([inner.astype(jnp.int32), jnp.array([0, SLOTS - 1], dtype=jnp.int32)])
    return jax.random.permutation(second_key, chosen).astype(jnp.int32)


def plant(values, key, least, largest):
    longest = values.shape.index(max(values.shape))
    spots = []
    for shift in (0, 1):
        where = [jax.random.randint(jax.random.fold_in(key, axis), (), 0, length) for axis, length in enumerate(values.shape)]
        where[longest] = (where[longest] + shift) % values.shape[longest]
        spots.append(tuple(where))
    return values.at[spots[0]].set(least).at[spots[1]].set(largest)


def levels(stream_key, dims, cuts, smallest, high):
    gain = 1.0
    for axis_at, shards_of in cuts:
        steps = jax.random.uniform(jax.random.fold_in(jax.random.fold_in(stream_key, 6), axis_at), (shards_of,), jnp.float32, smallest / len(cuts), high / len(cuts))
        gain = gain * jnp.repeat(jnp.exp(steps), dims[axis_at] // shards_of).reshape((-1,) + (1,) * (len(dims) - 1 - axis_at))
    return gain


def split_up(amount, total, limit, slope):
    weights = [(1 << 20) // math.isqrt(rank ** slope) + 1 for rank in range(2, amount + 1)]
    spare, holding = total - limit - (amount - 1), [1] * (amount - 1)
    while spare > 0:
        candidates = [i for i in range(amount - 1) if holding[i] < limit]
        pool, remaining = sum([weights[i] for i in candidates]), spare
        for i in candidates:
            more = min(limit - holding[i], max(1, remaining * weights[i] // pool), spare)
            holding[i] = holding[i] + more
            spare = spare - more
    return np.array([limit] + holding)


def ragged_sizes(key, number_of, total, limit, skew):
    if number_of == 2:
        one = jax.random.randint(key, (), max(1, total - limit), min(limit, total - 1) + 1)
        return jnp.stack([one, total - one])
    tallies = jnp.asarray(split_up(number_of, total, limit, skew), jnp.int32)
    pairs = (number_of - 1) // 2
    donor, sink = tallies[1:1 + 2 * pairs:2], tallies[2:2 + 2 * pairs:2]
    room = jnp.minimum(donor - 1, limit - sink)
    shifted = jax.random.randint(jax.random.fold_in(key, 1), (pairs,), 0, 1 << 20) % (room + 1)
    tallies = tallies.at[1:1 + 2 * pairs:2].set(donor - shifted).at[2:2 + 2 * pairs:2].set(sink + shifted)
    return tallies[jax.random.permutation(jax.random.fold_in(key, 2), number_of)]


def noise(rng, extent, spread, reach, pieces=(), kind=jnp.bfloat16):
    gain = levels(rng, extent, pieces, -0.22, 0.18) if pieces else 1.0
    entries = jax.random.normal(rng, extent, jnp.float32) * spread * gain
    return jnp.minimum(jnp.maximum(entries, -reach), reach).astype(kind)


def setup_inputs(seed: int = 0, part: int = 0) -> dict:
    streams_of = jax.random.split(jax.random.key(seed), 9)
    own_keys = jax.random.split(jax.random.fold_in(streams_of[8], part), 9)
    hidden = noise(own_keys[0], (TOTAL_ROWS, FF), 1.0, 6.0, ((0, 2), (1, 8)))
    residual = noise(own_keys[1], (TOTAL_ROWS, DOWN_WIDTH), 1.0, 6.0, ((0, 16),))
    down_weight = noise(streams_of[2], (FF, DOWN_WIDTH), FF ** -0.5, 0.03125, ((0, 8),))
    shrink_pool = noise(streams_of[3], (SLOTS, RANK, FF), FF ** -0.5, 0.03125, ((0, 2), (2, 8)))
    expand_pool = noise(streams_of[4], (SLOTS, RANK, DOWN_WIDTH), RANK ** -0.5, 0.75, ((0, 2), (2, 8)))
    seg_blocks = ragged_sizes(own_keys[5], SEGS, BLOCKS, SEG_MOST, 2).astype(jnp.int32)
    tail_rows = plant(jax.random.randint(own_keys[6], (SEGS,), 1, BLOCK + 1), jax.random.fold_in(own_keys[6], 1), 1, BLOCK).astype(jnp.int32)
    page_slot = draw_page_slot(jax.random.fold_in(jax.random.fold_in(streams_of[8], part), 71), part)
    return {"hidden": hidden, "residual": residual, "down_weight": down_weight, "shrink_pool": shrink_pool, "expand_pool": expand_pool, "seg_blocks": seg_blocks, "tail_rows": tail_rows, "page_slot": page_slot}


ADAPTER_SCALE = 0.5


def block_table(seg_blocks, tail_rows, page_slot, first_block, block_count, block_len):
    seg_ends = jnp.cumsum(seg_blocks, dtype=jnp.int32)
    block_ids = first_block + jnp.arange(block_count, dtype=jnp.int32)
    segment = jnp.sum((block_ids[:, None] >= seg_ends[None, :]).astype(jnp.int32), axis=1, dtype=jnp.int32)
    one_hot = (segment[:, None] == jnp.arange(seg_blocks.shape[0], dtype=jnp.int32)[None, :]).astype(jnp.int32)
    page_lookup = jnp.sum(one_hot * page_slot[None, :], axis=1, dtype=jnp.int32)
    last_block = jnp.sum(one_hot * seg_ends[None, :], axis=1, dtype=jnp.int32) - 1
    tail_of = jnp.sum(one_hot * tail_rows[None, :], axis=1, dtype=jnp.int32)
    active_rows = jnp.where(block_ids == last_block, tail_of, block_len).astype(jnp.int32)
    return page_lookup, active_rows


def reference(hidden, residual, down_weight, shrink_pool, expand_pool, seg_blocks, tail_rows, page_slot):
    page_lookup, active_rows = block_table(seg_blocks, tail_rows, page_slot, 0, BLOCKS, BLOCK)
    shard = FF // N_TP

    def add_shard(total, group):
        start = (group * shard).astype(jnp.int32)
        piece = lax.dynamic_slice_in_dim(hidden, start, shard, 1)
        weight_rows = lax.dynamic_slice_in_dim(down_weight, start, shard, 0)
        partial_sum = jnp.dot(piece, weight_rows, preferred_element_type=jnp.float32).astype(jnp.bfloat16)
        partial_sum = lax.optimization_barrier(partial_sum)
        return total + partial_sum.astype(jnp.float32), None

    base_output, _ = lax.scan(add_shard, jnp.zeros((TOTAL_ROWS, DOWN_WIDTH), jnp.float32), jnp.arange(N_TP, dtype=jnp.int32))
    block_list = hidden.reshape(BLOCKS, BLOCK, FF)

    def single_block(operands):
        block_rows, page_index, row_limit = operands
        rank_rows = jnp.dot(block_rows, shrink_pool[page_index].T, preferred_element_type=jnp.float32).astype(jnp.bfloat16)
        expanded_rows = jnp.dot(rank_rows, expand_pool[page_index], preferred_element_type=jnp.float32)
        active_row_mask = (jnp.arange(BLOCK, dtype=jnp.int32) < row_limit).astype(jnp.float32)
        return ADAPTER_SCALE * expanded_rows * active_row_mask[:, None]

    adapter_delta = lax.map(single_block, (block_list, page_lookup, active_rows)).reshape(TOTAL_ROWS, DOWN_WIDTH)
    return (residual.astype(jnp.float32) + base_output + adapter_delta).astype(jnp.bfloat16)
```

```python
import functools

import jax
import jax.numpy as jnp
from jax import lax
from jax.experimental import pallas as pl
from jax.experimental.pallas import tpu as pltpu
from jax.sharding import PartitionSpec as P

BLOCK = 128
ADAPTER_SCALE = 0.5
MESH = pl.DeviceIdType.MESH
F32 = jnp.float32
BF16 = jnp.bfloat16


def block_table(seg_blocks, tail_rows, page_slot, block_count, block_len):
    seg_ends = jnp.cumsum(seg_blocks, dtype=jnp.int32)
    block_ids = jnp.arange(block_count, dtype=jnp.int32)
    segment = jnp.sum(
        (block_ids[:, None] >= seg_ends[None, :]).astype(jnp.int32), axis=1, dtype=jnp.int32
    )
    one_hot = (
        segment[:, None] == jnp.arange(seg_blocks.shape[0], dtype=jnp.int32)[None, :]
    ).astype(jnp.int32)
    page_lookup = jnp.sum(one_hot * page_slot[None, :], axis=1, dtype=jnp.int32)
    last_block = jnp.sum(one_hot * seg_ends[None, :], axis=1, dtype=jnp.int32) - 1
    tail_of = jnp.sum(one_hot * tail_rows[None, :], axis=1, dtype=jnp.int32)
    active_rows = jnp.where(block_ids == last_block, tail_of, block_len)
    return (page_lookup, active_rows, one_hot)


def pick_kernel(index_ref, owned_ref, shrink_ref, expand_ref, s_ref, e_ref):
    owned = owned_ref[pl.program_id(0)] > 0
    s_ref[...] = jnp.where(owned, shrink_ref[...], jnp.zeros_like(shrink_ref))
    e_ref[...] = jnp.where(owned, expand_ref[...], jnp.zeros_like(expand_ref))


def pick_pages(index, owned, shrink_pool, expand_pool):
    segs = index.shape[0]
    _, rank, depth = shrink_pool.shape
    width = expand_pool.shape[2]
    return pl.pallas_call(
        pick_kernel,
        grid_spec=pltpu.PrefetchScalarGridSpec(
            num_scalar_prefetch=2,
            grid=(segs,),
            in_specs=[
                pl.BlockSpec((1, rank, depth), lambda i, idx, own: (idx[i], 0, 0)),
                pl.BlockSpec((1, rank, width), lambda i, idx, own: (idx[i], 0, 0)),
            ],
            out_specs=[
                pl.BlockSpec((1, rank, depth), lambda i, idx, own: (i, 0, 0)),
                pl.BlockSpec((1, rank, width), lambda i, idx, own: (i, 0, 0)),
            ],
        ),
        out_shape=[
            jax.ShapeDtypeStruct((segs, rank, depth), BF16),
            jax.ShapeDtypeStruct((segs, rank, width), BF16),
        ],
    )(index, owned, shrink_pool, expand_pool)


def main_kernel(
    tp, nz, tiles, rank,
    hid, weight, residual, s_own, e_own, oh, live, out,
    hv, wbuf, ysend, yrecv, keep, rr, ll, acc, s_mine, s_recv, e_recv, page, page_in,
    rk, rk_in, res_buf,
    hv_sem, w_sem, misc_sem, rep_send, rep_recv,
    y_send, y_recv, r_send, r_recv, l_send, l_recv,
    pg_send, pg_recv, rk_send, rk_recv,
):
    t = lax.axis_index("tp")
    rep = lax.axis_index("rep")
    z = t // 2
    y = t % 2
    across = z * 2 + (1 - y)
    c = wbuf.shape[2]
    depth = wbuf.shape[1]
    segs_rank = s_mine.shape[0]
    chunk = e_own.shape[1]
    per_chunk = chunk // c

    def w_copy(i):
        slot = lax.rem(i, 3)
        cols = pl.ds(pl.multiple_of(i * c, c), c)
        return pltpu.make_async_copy(weight.at[:, cols], wbuf.at[slot], w_sem.at[slot])

    def hv_copy(g):
        side = (1 - y) if g == 0 else y
        return pltpu.make_async_copy(hid.at[:, side], hv.at[g], hv_sem.at[g])

    hv_copy(0).start()
    w_copy(0).start()
    hv_copy(1).start()
    w_copy(1).start()
    s_copy = pltpu.make_async_copy(s_own, s_mine, misc_sem.at[0])
    res_copy = pltpu.make_async_copy(residual, res_buf, misc_sem.at[1])

    barrier = pltpu.get_barrier_semaphore()
    for j in range(1, tp):
        pl.semaphore_signal(
            barrier, inc=1, device_id={"tp": lax.rem(t + j, tp)}, device_id_type=MESH
        )
    pl.semaphore_signal(barrier, inc=1, device_id={"rep": 1 - rep}, device_id_type=MESH)
    pl.semaphore_wait(barrier, tp)

    e_swap = pltpu.make_async_remote_copy(
        src_ref=e_own, dst_ref=e_recv, send_sem=rep_send.at[0], recv_sem=rep_recv.at[0],
        device_id={"rep": 1 - rep}, device_id_type=MESH,
    )
    s_swap = pltpu.make_async_remote_copy(
        src_ref=s_own, dst_ref=s_recv, send_sem=rep_send.at[1], recv_sem=rep_recv.at[1],
        device_id={"rep": 1 - rep}, device_id_type=MESH,
    )
    e_swap.start()

    def y_copy(i):
        return pltpu.make_async_remote_copy(
            src_ref=ysend.at[i], dst_ref=yrecv.at[i],
            send_sem=y_send.at[i], recv_sem=y_recv.at[i],
            device_id={"tp": across}, device_id_type=MESH,
        )

    def right_copy(i, first, src):
        part = pl.ds(first, nz - first)
        return pltpu.make_async_remote_copy(
            src_ref=src.at[i, part], dst_ref=rr.at[i, part],
            send_sem=r_send.at[i], recv_sem=r_recv.at[i],
            device_id={"tp": lax.rem(t + 2, tp)}, device_id_type=MESH,
        )

    def left_copy(i, count, src):
        part = pl.ds(0, count)
        return pltpu.make_async_remote_copy(
            src_ref=src.at[i, part], dst_ref=ll.at[i, part],
            send_sem=l_send.at[i], recv_sem=l_recv.at[i],
            device_id={"tp": lax.rem(t + tp - 2, tp)}, device_id_type=MESH,
        )

    def product(g, w):
        value = jnp.dot(
            hv[g].reshape(nz * BLOCK, depth), w, preferred_element_type=F32
        )
        return value.astype(BF16).reshape(nz, BLOCK, c)

    def multiply(i):
        w_copy(i).wait()

        @pl.when(i + 2 < tiles)
        def _():
            w_copy(i + 2).start()

        slot = lax.rem(i, 3)
        ysend[i] = product(0, wbuf[slot])
        y_copy(i).start()

        @pl.when(i == 0)
        def _():
            hv_copy(1).wait()

        keep[i] = product(1, wbuf[slot])

    def add(i, d, other):
        return (keep[i, d].astype(F32) + other[i, d].astype(F32)).astype(BF16)

    def group(g):
        @pl.when(g < tiles)
        def _():
            y_copy(g).wait_recv()
            for d in range(nz):
                keep[g, d] = add(g, d, yrecv)

        for k in range(nz):
            i = g - k

            @pl.when((z == k) & (i >= 0) & (i < tiles))
            def _():
                if k > 0:
                    right_copy(i, k, keep).wait_recv()
                    for d in range(k + 1, nz):
                        rr[i, d] = add(i, d, rr)
                if k < nz - 1:
                    right_copy(i, k + 1, keep if k == 0 else rr).start()

            @pl.when((z == nz - 1 - k) & (i >= 0) & (i < tiles))
            def _():
                me = nz - 1 - k
                if k > 0:
                    left_copy(i, me + 1, keep).wait_recv()
                    for d in range(me):
                        ll[i, d] = add(i, d, ll)
                if me > 0:
                    left_copy(i, me, keep if k == 0 else ll).start()

        i = g - (nz - 1)

        @pl.when((i >= 0) & (i < tiles))
        def _():
            for k in range(nz):

                @pl.when(z == k)
                def _():
                    total = keep[i, k].astype(F32)
                    if k > 0:
                        total = total + rr[i, k].astype(F32)
                    if k < nz - 1:
                        total = total + ll[i, k].astype(F32)
                    acc[i] = total

    def page_copy(j):
        return pltpu.make_async_remote_copy(
            src_ref=page.at[lax.rem(t + j, tp)], dst_ref=page_in.at[j],
            send_sem=pg_send.at[j], recv_sem=pg_recv.at[j],
            device_id={"tp": lax.rem(t + j, tp)}, device_id_type=MESH,
        )

    def rank_copy(j):
        return pltpu.make_async_remote_copy(
            src_ref=rk.at[lax.rem(t + j, tp)], dst_ref=rk_in.at[j],
            send_sem=rk_send.at[j], recv_sem=rk_recv.at[j],
            device_id={"tp": lax.rem(t + j, tp)}, device_id_type=MESH,
        )

    def send_pages():
        e_swap.wait()
        row = lax.broadcasted_iota(jnp.int32, (rank, segs_rank), 0)
        col = lax.broadcasted_iota(jnp.int32, (rank, segs_rank), 1)
        diagonal = (lax.rem(col, rank) == row).astype(F32)
        both = e_own[...] + e_recv[...]

        @pl.loop(0, tp)
        def _(u):
            pick = (diagonal * oh[pl.ds(u, 1), :]).astype(BF16)
            page[u] = jnp.dot(pick, both, preferred_element_type=F32).astype(BF16)

        for j in range(1, tp):
            page_copy(j).start()

    def send_ranks():
        s_copy.wait()
        s_swap.wait()
        s_mine[...] = s_mine[...] + s_recv[...]
        row = lax.broadcasted_iota(jnp.int32, (segs_rank, BLOCK), 0)
        col = lax.broadcasted_iota(jnp.int32, (segs_rank, BLOCK), 1)
        fold = (lax.rem(row, rank) == col).astype(BF16)
        for g in range(2):
            side = (1 - y) if g == 0 else y
            sums = lax.dot_general(
                hv[g].reshape(nz * BLOCK, depth), s_mine[...], (((1,), (1,)), ((), ())),
                preferred_element_type=F32,
            )
            for d in range(nz):
                u = 2 * d + side
                chosen = (sums[d * BLOCK : (d + 1) * BLOCK] * oh[pl.ds(u, 1), :]).astype(BF16)
                rk[u] = jnp.dot(chosen, fold, preferred_element_type=F32).astype(BF16)
        for j in range(1, tp):
            rank_copy(j).start()

    def add_delta():
        total = rk[t].astype(F32)
        for j in range(1, tp):
            rank_copy(j).wait()
            total = total + rk_in[j].astype(F32)
        rows = (total.astype(BF16).astype(F32) * live[...]).astype(BF16)[:, :rank]
        res_copy.wait()
        for j in range(tp):
            if j > 0:
                page_copy(j).wait()
                factor = page_in[j]
            else:
                factor = page[t]
            delta = jnp.dot(rows, factor, preferred_element_type=F32)
            owner = lax.rem(t + tp - j, tp)
            for h in range(per_chunk):
                tile = owner * per_chunk + h
                cols = pl.ds(pl.multiple_of(tile * c, c), c)
                acc[tile] = acc[tile] + delta[:, h * c : (h + 1) * c]

    hv_copy(0).wait()
    half = tiles // 2

    @pl.loop(0, half)
    def _(i):
        multiply(2 * i)
        multiply(2 * i + 1)

        @pl.when(i == 0)
        def _():
            send_pages()
            s_swap.start()
            s_copy.start()
            res_copy.start()

        @pl.when(i > 0)
        def _():
            group(i - 1)

    send_ranks()

    @pl.loop(half - 1, tiles + nz - 1)
    def _(g):
        group(g)

    add_delta()
    for i in range(tiles):
        cols = slice(i * c, (i + 1) * c)
        out[:, cols] = (res_buf[:, cols].astype(F32) + acc[i]).astype(BF16)

    @pl.loop(0, tiles)
    def _(i):
        y_copy(i).wait_send()
        for k in range(nz):

            @pl.when(z == k)
            def _():
                if k < nz - 1:
                    right_copy(i, k + 1, rr).wait_send()
                if k > 0:
                    left_copy(i, k, ll).wait_send()


def fused(tp, rank, hidden, weight, residual, s_own, e_own, oh, live):
    rows, depth = hidden.shape
    width = weight.shape[1]
    nz = tp // 2
    c = min(256, e_own.shape[1])
    tiles = width // c
    segs_rank, chunk = e_own.shape
    hid = hidden.reshape(nz, 2, BLOCK, depth)
    hbm = pl.BlockSpec(memory_space=pl.ANY)
    vmem = pl.BlockSpec(memory_space=pltpu.VMEM)
    slab = pltpu.VMEM((tiles, nz, BLOCK, c), BF16)
    dma = pltpu.SemaphoreType.DMA
    return pl.pallas_call(
        functools.partial(main_kernel, tp, nz, tiles, rank),
        out_shape=jax.ShapeDtypeStruct((BLOCK, width), BF16),
        in_specs=[hbm, hbm, hbm, hbm, vmem, vmem, vmem],
        out_specs=vmem,
        scratch_shapes=[
            pltpu.VMEM((2, nz, BLOCK, depth), BF16),
            pltpu.VMEM((3, depth, c), BF16),
            slab, slab, slab, slab, slab,
            pltpu.VMEM((tiles, BLOCK, c), F32),
            pltpu.VMEM((segs_rank, depth), BF16),
            pltpu.VMEM((segs_rank, depth), BF16),
            pltpu.VMEM((segs_rank, chunk), BF16),
            pltpu.VMEM((tp, rank, chunk), BF16),
            pltpu.VMEM((tp, rank, chunk), BF16),
            pltpu.VMEM((tp, BLOCK, BLOCK), BF16),
            pltpu.VMEM((tp, BLOCK, BLOCK), BF16),
            pltpu.VMEM((BLOCK, width), BF16),
            dma((2,)), dma((3,)), dma((2,)), dma((2,)), dma((2,)),
            dma((tiles,)), dma((tiles,)), dma((tiles,)), dma((tiles,)), dma((tiles,)),
            dma((tiles,)),
            dma((tp,)), dma((tp,)), dma((tp,)), dma((tp,)),
        ],
        compiler_params=pltpu.CompilerParams(
            collective_id=0, has_side_effects=True, vmem_limit_bytes=60 * 1024 * 1024
        ),
        cost_estimate=pl.CostEstimate(
            flops=2 * rows * depth * (width + segs_rank),
            bytes_accessed=2 * depth * (width + rows),
            transcendentals=0,
        ),
    )(hid, weight, residual, s_own, e_own, oh, live)


def body_fused(hidden, residual, down_weight, shrink_pool, expand_pool, seg_blocks, tail_rows, page_slot):
    rep_count = lax.axis_size("rep")
    tp_count = lax.axis_size("tp")
    rep_index = lax.axis_index("rep")
    tp_index = lax.axis_index("tp")
    blk_rep = hidden.shape[0] // BLOCK
    pages_here, rank, depth = shrink_pool.shape
    segs = seg_blocks.shape[0]
    local = page_slot - rep_index * pages_here
    owned = ((local >= 0) & (local < pages_here)).astype(jnp.int32)
    local = jnp.clip(local, 0, pages_here - 1)
    s_own, e_own = pick_pages(local, owned, shrink_pool, expand_pool)
    _, every_live, one_hot = block_table(
        seg_blocks, tail_rows, page_slot, rep_count * blk_rep, BLOCK
    )
    one_hot = lax.dynamic_slice_in_dim(one_hot, rep_index * blk_rep, blk_rep, 0)
    oh = jnp.repeat(one_hot.astype(F32), rank, axis=1)
    live_rows = lax.dynamic_index_in_dim(
        every_live, rep_index * blk_rep + tp_index, 0, keepdims=False
    )
    row_ids = lax.broadcasted_iota(jnp.int32, (BLOCK, BLOCK), 0)
    live = jnp.where(row_ids < live_rows, ADAPTER_SCALE, 0.0).astype(F32)
    return fused(
        tp_count, rank, hidden, down_weight, residual,
        s_own.reshape(segs * rank, depth), e_own.reshape(segs * rank, -1), oh, live,
    )


def body_plain(hidden, residual, down_weight, shrink_pool, expand_pool, seg_blocks, tail_rows, page_slot):
    rep_count = lax.axis_size("rep")
    rep_index = lax.axis_index("rep")
    repeated_rows = hidden.shape[0]
    blk_rep = repeated_rows // BLOCK
    every_page, every_live, _ = block_table(
        seg_blocks, tail_rows, page_slot, rep_count * blk_rep, BLOCK
    )
    page_lookup = lax.dynamic_slice_in_dim(every_page, rep_index * blk_rep, blk_rep, 0)
    active_rows = lax.dynamic_slice_in_dim(every_live, rep_index * blk_rep, blk_rep, 0)
    all_shrink = lax.all_gather(shrink_pool, "rep", axis=0, tiled=True)
    all_expand = lax.all_gather(expand_pool, "rep", axis=0, tiled=True)
    shrink_pages = jnp.take(all_shrink, page_lookup, axis=0)
    expand_pages = jnp.take(all_expand, page_lookup, axis=0)
    block_list = hidden.reshape(blk_rep, BLOCK, hidden.shape[1])
    shrink_part = jnp.einsum("bnf,bkf->bnk", block_list, shrink_pages, preferred_element_type=F32)
    rank_rows = lax.psum(shrink_part.astype(BF16), "tp")
    expanded = jnp.einsum("bnk,bkc->bnc", rank_rows, expand_pages, preferred_element_type=F32)
    mask = (jnp.arange(BLOCK, dtype=jnp.int32)[None, :] < active_rows[:, None]).astype(F32)
    delta = (ADAPTER_SCALE * expanded * mask[:, :, None]).reshape(repeated_rows, -1)
    partial = jnp.dot(hidden, down_weight, preferred_element_type=F32).astype(BF16)
    total = lax.psum_scatter(partial, "tp", scatter_dimension=0, tiled=True).astype(F32)
    total = total + lax.all_to_all(
        delta.astype(BF16), "tp", split_axis=0, concat_axis=1, tiled=True
    ).astype(F32)
    return (residual.astype(F32) + total).astype(BF16)


def body(hidden, residual, *rest):
    tp_count = lax.axis_size("tp")
    pairs = lax.axis_size("rep") == 2 and tp_count in (4, 6, 8)
    if pairs and residual.shape[0] == BLOCK and hidden.shape[0] == tp_count * BLOCK:
        return body_fused(hidden, residual, *rest)
    return body_plain(hidden, residual, *rest)


def solution(mesh):
    return jax.shard_map(
        body,
        mesh=mesh,
        in_specs=(
            P(("parts", "rep"), "tp"),
            P(("parts", "rep", "tp"), None),
            P("tp", None),
            P("rep", None, "tp"),
            P("rep", None, "tp"),
            P("parts"),
            P("parts"),
            P("parts"),
        ),
        out_specs=P(("parts", "rep", "tp"), None),
        check_vma=False,
    )
```

```python
import functools

import jax
import jax.numpy as jnp
from jax import lax
from jax.experimental import pallas as pl
from jax.experimental.pallas import tpu as pltpu
from jax.sharding import PartitionSpec as P

BLOCK = 128
ADAPTER_SCALE = 0.5
MESH = pl.DeviceIdType.MESH
F32 = jnp.float32
BF16 = jnp.bfloat16


def block_table(seg_blocks, tail_rows, page_slot, block_count, block_len):
    seg_ends = jnp.cumsum(seg_blocks, dtype=jnp.int32)
    block_ids = jnp.arange(block_count, dtype=jnp.int32)
    segment = jnp.sum(
        (block_ids[:, None] >= seg_ends[None, :]).astype(jnp.int32), axis=1, dtype=jnp.int32
    )
    one_hot = (
        segment[:, None] == jnp.arange(seg_blocks.shape[0], dtype=jnp.int32)[None, :]
    ).astype(jnp.int32)
    page_lookup = jnp.sum(one_hot * page_slot[None, :], axis=1, dtype=jnp.int32)
    last_block = jnp.sum(one_hot * seg_ends[None, :], axis=1, dtype=jnp.int32) - 1
    tail_of = jnp.sum(one_hot * tail_rows[None, :], axis=1, dtype=jnp.int32)
    active_rows = jnp.where(block_ids == last_block, tail_of, block_len)
    return (page_lookup, active_rows, one_hot)


def pick_kernel(
    tp, seg_ref, tail_ref, slot_ref, shrink, expand, s_out, e_out, oh_ref, own_ref, live_ref, s_sem, e_sem
):
    rep = lax.axis_index("rep")
    mine = rep * tp + lax.axis_index("tp")
    pages_here, rank, _ = shrink.shape
    segs = s_out.shape[0]
    copies = []
    for s in range(segs):
        local = slot_ref[s] - rep * pages_here
        local = jnp.minimum(jnp.maximum(local, 0), pages_here - 1)
        copies.append(pltpu.make_async_copy(shrink.at[local], s_out.at[s], s_sem.at[s]))
        copies.append(pltpu.make_async_copy(expand.at[local], e_out.at[s], e_sem.at[s]))
    for copy in copies:
        copy.start()
    block = lax.broadcasted_iota(jnp.int32, oh_ref.shape, 0) + rep * tp
    group = lax.broadcasted_iota(jnp.int32, oh_ref.shape, 1) // rank
    own_group = lax.broadcasted_iota(jnp.int32, own_ref.shape, 0) // rank
    oh = jnp.zeros(oh_ref.shape, F32)
    own = jnp.zeros(own_ref.shape, F32)
    limit = jnp.int32(BLOCK)
    begin = jnp.int32(0)
    for s in range(segs):
        end = begin + seg_ref[s]
        oh = jnp.where((group == s) & (block >= begin) & (block < end), 1.0, oh)
        local = slot_ref[s] - rep * pages_here
        here = jnp.where((local >= 0) & (local < pages_here), 1.0, 0.0)
        own = jnp.where(own_group == s, here, own)
        limit = jnp.where(mine == end - 1, tail_ref[s], limit)
        begin = end
    oh_ref[...] = oh
    own_ref[...] = own
    row = lax.broadcasted_iota(jnp.int32, live_ref.shape, 0)
    live_ref[...] = jnp.where(row < limit, ADAPTER_SCALE, 0.0)
    for copy in copies:
        copy.wait()


def pick_pages(tp, seg_blocks, tail_rows, page_slot, shrink_pool, expand_pool):
    segs = seg_blocks.shape[0]
    _, rank, depth = shrink_pool.shape
    width = expand_pool.shape[2]
    smem = pl.BlockSpec(memory_space=pltpu.SMEM)
    hbm = pl.BlockSpec(memory_space=pl.ANY)
    vmem = pl.BlockSpec(memory_space=pltpu.VMEM)
    return pl.pallas_call(
        functools.partial(pick_kernel, tp),
        in_specs=[smem, smem, smem, hbm, hbm],
        out_specs=[hbm, hbm, vmem, vmem, vmem],
        out_shape=[
            jax.ShapeDtypeStruct((segs, rank, depth), BF16),
            jax.ShapeDtypeStruct((segs, rank, width), BF16),
            jax.ShapeDtypeStruct((tp, segs * rank), F32),
            jax.ShapeDtypeStruct((segs * rank, 128), F32),
            jax.ShapeDtypeStruct((BLOCK, rank), F32),
        ],
        scratch_shapes=[pltpu.SemaphoreType.DMA((segs,)), pltpu.SemaphoreType.DMA((segs,))],
    )(seg_blocks, tail_rows, page_slot, shrink_pool, expand_pool)


def main_kernel(
    tp, nz, tiles, nb, rank,
    hid, weight, residual, s_own, e_own, oh, own, live, out,
    hv, wbuf, ysend, yrecv, keep, rr, ll, keep_b, rr_b, ll_b, ysend_b, yrecv_b,
    acc, delta_buf, s_mine, s_recv, e_recv, page, page_in,
    rk, rk_in, res_buf, e_mine,
    hv_sem, w_sem, misc_sem, rep_send, rep_recv,
    y_send, y_recv, r_send, r_recv, l_send, l_recv,
    yb_send, yb_recv, rb_send, rb_recv, lb_send, lb_recv,
    pg_send, pg_recv, rk_send, rk_recv,
):
    t = lax.axis_index("tp")
    rep = lax.axis_index("rep")
    z = t // 2
    y = t % 2
    across = z * 2 + (1 - y)
    c = wbuf.shape[2]
    depth = wbuf.shape[1]
    segs_rank = s_mine.shape[0]
    chunk = e_own.shape[1]
    per_chunk = chunk // c
    na = tiles - nb

    def w_copy(i):
        slot = lax.rem(i, 3)
        cols = pl.ds(pl.multiple_of(i * c, c), c)
        return pltpu.make_async_copy(weight.at[:, cols], wbuf.at[slot], w_sem.at[slot])

    def hv_copy(g):
        side = (1 - y) if g == 0 else y
        return pltpu.make_async_copy(hid.at[:, side], hv.at[g], hv_sem.at[g])

    hv_copy(0).start()
    w_copy(0).start()
    hv_copy(1).start()
    w_copy(1).start()
    s_copy = pltpu.make_async_copy(s_own, s_mine, misc_sem.at[0])
    e_copy = pltpu.make_async_copy(e_own, e_mine, misc_sem.at[2])
    e_copy.start()
    res_copy = pltpu.make_async_copy(residual, res_buf, misc_sem.at[1])

    barrier = pltpu.get_barrier_semaphore()
    for j in range(1, tp):
        pl.semaphore_signal(
            barrier, inc=1, device_id={"tp": lax.rem(t + j, tp)}, device_id_type=MESH
        )
    pl.semaphore_signal(barrier, inc=1, device_id={"rep": 1 - rep}, device_id_type=MESH)
    pl.semaphore_wait(barrier, tp)

    e_swap = pltpu.make_async_remote_copy(
        src_ref=e_own, dst_ref=e_recv, send_sem=rep_send.at[0], recv_sem=rep_recv.at[0],
        device_id={"rep": 1 - rep}, device_id_type=MESH,
    )
    s_swap = pltpu.make_async_remote_copy(
        src_ref=s_own, dst_ref=s_recv, send_sem=rep_send.at[1], recv_sem=rep_recv.at[1],
        device_id={"rep": 1 - rep}, device_id_type=MESH,
    )
    e_swap.start()

    def y_copy(i):
        return pltpu.make_async_remote_copy(
            src_ref=ysend.at[i], dst_ref=yrecv.at[i],
            send_sem=y_send.at[i], recv_sem=y_recv.at[i],
            device_id={"tp": across}, device_id_type=MESH,
        )

    def right_copy(i, first, src):
        part = pl.ds(first, nz - first)
        return pltpu.make_async_remote_copy(
            src_ref=src.at[i, part], dst_ref=rr.at[i, part],
            send_sem=r_send.at[i], recv_sem=r_recv.at[i],
            device_id={"tp": lax.rem(t + 2, tp)}, device_id_type=MESH,
        )

    def left_copy(i, count, src):
        part = pl.ds(0, count)
        return pltpu.make_async_remote_copy(
            src_ref=src.at[i, part], dst_ref=ll.at[i, part],
            send_sem=l_send.at[i], recv_sem=l_recv.at[i],
            device_id={"tp": lax.rem(t + tp - 2, tp)}, device_id_type=MESH,
        )

    def y_copy_b(b):
        return pltpu.make_async_remote_copy(
            src_ref=ysend_b.at[b], dst_ref=yrecv_b.at[b],
            send_sem=yb_send.at[b], recv_sem=yb_recv.at[b],
            device_id={"tp": across}, device_id_type=MESH,
        )

    def right_copy_b(b, first, src):
        part = pl.ds(first, nz - first)
        return pltpu.make_async_remote_copy(
            src_ref=src.at[b, :, part], dst_ref=rr_b.at[b, :, part],
            send_sem=rb_send.at[b], recv_sem=rb_recv.at[b],
            device_id={"tp": lax.rem(t + 2, tp)}, device_id_type=MESH,
        )

    def left_copy_b(b, count, src):
        part = pl.ds(0, count)
        return pltpu.make_async_remote_copy(
            src_ref=src.at[b, :, part], dst_ref=ll_b.at[b, :, part],
            send_sem=lb_send.at[b], recv_sem=lb_recv.at[b],
            device_id={"tp": lax.rem(t + tp - 2, tp)}, device_id_type=MESH,
        )

    def product(g, w):
        value = jnp.dot(
            hv[g].reshape(nz * BLOCK, depth), w, preferred_element_type=F32
        )
        return value.astype(BF16).reshape(nz, BLOCK, c)

    def next_weight(i):
        w_copy(i).wait()

        @pl.when(i + 2 < tiles)
        def _():
            w_copy(i + 2).start()

        return lax.rem(i, 3)

    def multiply(i, a):
        slot = next_weight(i)
        ysend[a] = product(0, wbuf[slot])
        y_copy(a).start()

        @pl.when(i == 0)
        def _():
            hv_copy(1).wait()

        keep[a] = product(1, wbuf[slot])

    def multiply_b(i, b):
        slot = next_weight(i)
        for g in range(2):
            keep_b[b, g] = product(g, wbuf[slot])

    def add(i, d, other):
        return (keep[i, d].astype(F32) + other[i, d].astype(F32)).astype(BF16)

    def group(g):
        @pl.when((g >= 0) & (g < na))
        def _():
            y_copy(g).wait_recv()
            for d in range(nz):
                keep[g, d] = add(g, d, yrecv)

        for k in range(nz):
            i = g - k

            @pl.when((z == k) & (i >= 0) & (i < na))
            def _():
                if k > 0:
                    right_copy(i, k, keep).wait_recv()
                    for d in range(k + 1, nz):
                        rr[i, d] = add(i, d, rr)
                if k < nz - 1:
                    right_copy(i, k + 1, keep if k == 0 else rr).start()

            @pl.when((z == nz - 1 - k) & (i >= 0) & (i < na))
            def _():
                me = nz - 1 - k
                if k > 0:
                    left_copy(i, me + 1, keep).wait_recv()
                    for d in range(me):
                        ll[i, d] = add(i, d, ll)
                if me > 0:
                    left_copy(i, me, keep if k == 0 else ll).start()

        i = g - (nz - 1)

        @pl.when((i >= 0) & (i < na))
        def _():
            for k in range(nz):

                @pl.when(z == k)
                def _():
                    total = keep[i, k].astype(F32)
                    if k > 0:
                        total = total + rr[i, k].astype(F32)
                    if k < nz - 1:
                        total = total + ll[i, k].astype(F32)
                    acc[jnp.where(i < nb, 2 * i, i + nb)] = total

    def add_b(b, g, d, other):
        return (keep_b[b, g, d].astype(F32) + other[b, g, d].astype(F32)).astype(BF16)

    def group_b(i):
        for k in range(nz):
            b = i - 2 * k

            @pl.when((z == k) & (b >= 0) & (b < nb))
            def _():
                if k > 0:
                    right_copy_b(b, k, keep_b).wait_recv()
                    for g in range(2):
                        for d in range(k + 1, nz):
                            rr_b[b, g, d] = add_b(b, g, d, rr_b)
                if k < nz - 1:
                    right_copy_b(b, k + 1, keep_b if k == 0 else rr_b).start()

            @pl.when((z == nz - 1 - k) & (b >= 0) & (b < nb))
            def _():
                me = nz - 1 - k
                if k > 0:
                    left_copy_b(b, me + 1, keep_b).wait_recv()
                    for g in range(2):
                        for d in range(me):
                            ll_b[b, g, d] = add_b(b, g, d, ll_b)
                if me > 0:
                    left_copy_b(b, me, keep_b if k == 0 else ll_b).start()

        b = i - 2 * (nz - 1)

        @pl.when((b >= 0) & (b < nb))
        def _():
            for k in range(nz):

                @pl.when(z == k)
                def _():
                    for g in range(2):
                        total = keep_b[b, g, k].astype(F32)
                        if k > 0:
                            total = total + rr_b[b, g, k].astype(F32)
                        if k < nz - 1:
                            total = total + ll_b[b, g, k].astype(F32)
                        if g == 0:
                            ysend_b[b] = total.astype(BF16)
                        else:
                            acc[2 * b + 1] = total

            y_copy_b(b).start()

        last = i - 2 * nz

        @pl.when((last >= 0) & (last < nb))
        def _():
            y_copy_b(last).wait_recv()
            acc[2 * last + 1] = acc[2 * last + 1] + yrecv_b[last].astype(F32)

    def page_copy(j):
        return pltpu.make_async_remote_copy(
            src_ref=page.at[lax.rem(t + j, tp)], dst_ref=page_in.at[j],
            send_sem=pg_send.at[j], recv_sem=pg_recv.at[j],
            device_id={"tp": lax.rem(t + j, tp)}, device_id_type=MESH,
        )

    def rank_copy(j):
        return pltpu.make_async_remote_copy(
            src_ref=rk.at[lax.rem(t + j, tp)], dst_ref=rk_in.at[j],
            send_sem=rk_send.at[j], recv_sem=rk_recv.at[j],
            device_id={"tp": lax.rem(t + j, tp)}, device_id_type=MESH,
        )

    def send_pages():
        e_copy.wait()
        e_swap.wait()
        row = lax.broadcasted_iota(jnp.int32, (rank, segs_rank), 0)
        col = lax.broadcasted_iota(jnp.int32, (rank, segs_rank), 1)
        diagonal = (lax.rem(col, rank) == row).astype(F32)
        is_own = jnp.concatenate([own[...].astype(BF16)] * (chunk // 128), axis=1)
        both = e_mine[...] * is_own + e_recv[...] * (1 - is_own)

        @pl.loop(0, tp)
        def _(u):
            pick = (diagonal * oh[pl.ds(u, 1), :]).astype(BF16)
            page[u] = jnp.dot(pick, both, preferred_element_type=F32).astype(BF16)

        for j in range(1, tp):
            page_copy(j).start()

    def join_shrink():
        s_copy.wait()
        s_swap.wait()
        is_own = own[...].astype(BF16)

        @pl.loop(0, depth // 128)
        def _(i):
            cols = pl.ds(pl.multiple_of(i * 128, 128), 128)
            s_mine[:, cols] = s_mine[:, cols] * is_own + s_recv[:, cols] * (1 - is_own)

    def rank_sums(g):
        half_rows = BLOCK // 2
        row = lax.rem(lax.broadcasted_iota(jnp.int32, (segs_rank, 2 * rank), 0), rank)
        col = lax.broadcasted_iota(jnp.int32, (segs_rank, 2 * rank), 1)
        top = (row == col).astype(BF16)
        low = (row + rank == col).astype(BF16)
        side = (1 - y) if g == 0 else y
        sums = lax.dot_general(
            hv[g].reshape(nz * BLOCK, depth), s_mine[...], (((1,), (1,)), ((), ())),
            preferred_element_type=F32,
        )
        for d in range(nz):
            u = 2 * d + side
            chosen = (sums[d * BLOCK : (d + 1) * BLOCK] * oh[pl.ds(u, 1), :]).astype(BF16)
            rk[u] = (
                jnp.dot(chosen[:half_rows], top, preferred_element_type=F32)
                + jnp.dot(chosen[half_rows:], low, preferred_element_type=F32)
            ).astype(BF16)

    def add_delta():
        total = rk[t].astype(F32)
        for j in range(1, tp):
            rank_copy(j).wait()
            total = total + rk_in[j].astype(F32)
        total = total.astype(BF16)
        row = lax.broadcasted_iota(jnp.int32, (2 * rank, rank), 0)
        col = lax.broadcasted_iota(jnp.int32, (2 * rank, rank), 1)
        rows = jnp.concatenate(
            [
                jnp.dot(total, (row == col).astype(BF16), preferred_element_type=F32),
                jnp.dot(total, (row == col + rank).astype(BF16), preferred_element_type=F32),
            ],
            axis=0,
        )
        rows = (rows * live[...]).astype(BF16)
        for j in range(tp):
            if j > 0:
                page_copy(j).wait()
                factor = page_in[j]
            else:
                factor = page[t]
            delta = jnp.dot(rows, factor, preferred_element_type=F32)
            owner = lax.rem(t + tp - j, tp)
            for h in range(per_chunk):
                delta_buf[owner * per_chunk + h] = delta[:, h * c : (h + 1) * c]
        res_copy.wait()
        for i in range(tiles):
            delta_buf[i] = delta_buf[i] + res_buf[:, i * c : (i + 1) * c].astype(F32)

    send_pages()
    hv_copy(0).wait()
    half = tiles // 2

    @pl.loop(0, half)
    def _(i):
        @pl.when(i < nb)
        def _():
            multiply(2 * i, i)
            multiply_b(2 * i + 1, i)

        @pl.when(i >= nb)
        def _():
            multiply(2 * i, 2 * i - nb)
            multiply(2 * i + 1, 2 * i + 1 - nb)

        @pl.when(i == 0)
        def _():
            s_swap.start()
            s_copy.start()
            res_copy.start()

        group_b(i)
        group(i - 1)

        @pl.when(i == half - 3)
        def _():
            join_shrink()
            rank_sums(0)

        @pl.when(i == half - 2)
        def _():
            rank_sums(1)
            for j in range(1, tp):
                rank_copy(j).start()

    steps = max(na + nz, nb + 2 * nz)
    middle = (half + steps) // 2

    @pl.loop(half, middle)
    def _(i):
        group_b(i)
        group(i - 1)

    add_delta()

    @pl.loop(middle, steps)
    def _(i):
        group_b(i)
        group(i - 1)

    for i in range(tiles):
        out[:, i * c : (i + 1) * c] = (delta_buf[i] + acc[i]).astype(BF16)

    @pl.loop(0, na)
    def _(i):
        y_copy(i).wait_send()
        for k in range(nz):

            @pl.when(z == k)
            def _():
                if k < nz - 1:
                    right_copy(i, k + 1, rr).wait_send()
                if k > 0:
                    left_copy(i, k, ll).wait_send()

    @pl.loop(0, nb)
    def _(b):
        y_copy_b(b).wait_send()
        for k in range(nz):

            @pl.when(z == k)
            def _():
                if k < nz - 1:
                    right_copy_b(b, k + 1, rr_b).wait_send()
                if k > 0:
                    left_copy_b(b, k, ll_b).wait_send()


def fused(tp, rank, hidden, weight, residual, s_own, e_own, oh, own, live):
    rows, depth = hidden.shape
    width = weight.shape[1]
    nz = tp // 2
    c = min(256, e_own.shape[1])
    tiles = width // c
    segs_rank, chunk = e_own.shape
    hid = hidden.reshape(nz, 2, BLOCK, depth)
    hbm = pl.BlockSpec(memory_space=pl.ANY)
    vmem = pl.BlockSpec(memory_space=pltpu.VMEM)
    nb = (3 * tiles) // 16
    na = tiles - nb
    slab = pltpu.VMEM((na, nz, BLOCK, c), BF16)
    slab_b = pltpu.VMEM((nb, 2, nz, BLOCK, c), BF16)
    row_b = pltpu.VMEM((nb, BLOCK, c), BF16)
    dma = pltpu.SemaphoreType.DMA
    return pl.pallas_call(
        functools.partial(main_kernel, tp, nz, tiles, nb, rank),
        out_shape=jax.ShapeDtypeStruct((BLOCK, width), BF16),
        in_specs=[hbm, hbm, hbm, hbm, hbm, vmem, vmem, vmem],
        out_specs=vmem,
        scratch_shapes=[
            pltpu.VMEM((2, nz, BLOCK, depth), BF16),
            pltpu.VMEM((3, depth, c), BF16),
            slab, slab, slab, slab, slab,
            slab_b, slab_b, slab_b, row_b, row_b,
            pltpu.VMEM((tiles, BLOCK, c), F32),
            pltpu.VMEM((tiles, BLOCK, c), F32),
            pltpu.VMEM((segs_rank, depth), BF16),
            pltpu.VMEM((segs_rank, depth), BF16),
            pltpu.VMEM((segs_rank, chunk), BF16),
            pltpu.VMEM((tp, rank, chunk), BF16),
            pltpu.VMEM((tp, rank, chunk), BF16),
            pltpu.VMEM((tp, BLOCK // 2, 2 * rank), BF16),
            pltpu.VMEM((tp, BLOCK // 2, 2 * rank), BF16),
            pltpu.VMEM((BLOCK, width), BF16),
            pltpu.VMEM((segs_rank, chunk), BF16),
            dma((2,)), dma((3,)), dma((3,)), dma((2,)), dma((2,)),
            dma((na,)), dma((na,)), dma((na,)), dma((na,)), dma((na,)), dma((na,)),
            dma((nb,)), dma((nb,)), dma((nb,)), dma((nb,)), dma((nb,)), dma((nb,)),
            dma((tp,)), dma((tp,)), dma((tp,)), dma((tp,)),
        ],
        compiler_params=pltpu.CompilerParams(
            collective_id=0, has_side_effects=True, vmem_limit_bytes=60 * 1024 * 1024
        ),
        cost_estimate=pl.CostEstimate(
            flops=2 * rows * depth * (width + segs_rank),
            bytes_accessed=2 * depth * (width + rows),
            transcendentals=0,
        ),
    )(hid, weight, residual, s_own, e_own, oh, own, live)


def body_fused(hidden, residual, down_weight, shrink_pool, expand_pool, seg_blocks, tail_rows, page_slot):
    tp_count = lax.axis_size("tp")
    segs = seg_blocks.shape[0]
    _, rank, depth = shrink_pool.shape
    s_own, e_own, oh, own, live = pick_pages(
        tp_count, seg_blocks, tail_rows, page_slot, shrink_pool, expand_pool
    )
    return fused(
        tp_count, rank, hidden, down_weight, residual,
        s_own.reshape(segs * rank, depth), e_own.reshape(segs * rank, -1), oh, own, live,
    )


def body_plain(hidden, residual, down_weight, shrink_pool, expand_pool, seg_blocks, tail_rows, page_slot):
    rep_count = lax.axis_size("rep")
    rep_index = lax.axis_index("rep")
    repeated_rows = hidden.shape[0]
    blk_rep = repeated_rows // BLOCK
    every_page, every_live, _ = block_table(
        seg_blocks, tail_rows, page_slot, rep_count * blk_rep, BLOCK
    )
    page_lookup = lax.dynamic_slice_in_dim(every_page, rep_index * blk_rep, blk_rep, 0)
    active_rows = lax.dynamic_slice_in_dim(every_live, rep_index * blk_rep, blk_rep, 0)
    all_shrink = lax.all_gather(shrink_pool, "rep", axis=0, tiled=True)
    all_expand = lax.all_gather(expand_pool, "rep", axis=0, tiled=True)
    shrink_pages = jnp.take(all_shrink, page_lookup, axis=0)
    expand_pages = jnp.take(all_expand, page_lookup, axis=0)
    block_list = hidden.reshape(blk_rep, BLOCK, hidden.shape[1])
    shrink_part = jnp.einsum("bnf,bkf->bnk", block_list, shrink_pages, preferred_element_type=F32)
    rank_rows = lax.psum(shrink_part.astype(BF16), "tp")
    expanded = jnp.einsum("bnk,bkc->bnc", rank_rows, expand_pages, preferred_element_type=F32)
    mask = (jnp.arange(BLOCK, dtype=jnp.int32)[None, :] < active_rows[:, None]).astype(F32)
    delta = (ADAPTER_SCALE * expanded * mask[:, :, None]).reshape(repeated_rows, -1)
    partial = jnp.dot(hidden, down_weight, preferred_element_type=F32).astype(BF16)
    total = lax.psum_scatter(partial, "tp", scatter_dimension=0, tiled=True).astype(F32)
    total = total + lax.all_to_all(
        delta.astype(BF16), "tp", split_axis=0, concat_axis=1, tiled=True
    ).astype(F32)
    return (residual.astype(F32) + total).astype(BF16)


def body(hidden, residual, down_weight, shrink_pool, *rest):
    tp_count = lax.axis_size("tp")
    pairs = lax.axis_size("rep") == 2 and tp_count in (4, 6, 8)
    pairs = pairs and 2 * shrink_pool.shape[1] == BLOCK
    if pairs and residual.shape[0] == BLOCK and hidden.shape[0] == tp_count * BLOCK:
        return body_fused(hidden, residual, down_weight, shrink_pool, *rest)
    return body_plain(hidden, residual, down_weight, shrink_pool, *rest)


def solution(mesh):
    return jax.shard_map(
        body,
        mesh=mesh,
        in_specs=(
            P(("parts", "rep"), "tp"),
            P(("parts", "rep", "tp"), None),
            P("tp", None),
            P("rep", None, "tp"),
            P("rep", None, "tp"),
            P("parts"),
            P("parts"),
            P("parts"),
        ),
        out_specs=P(("parts", "rep", "tp"), None),
        check_vma=False,
    )
```

```python
import functools

import jax
import jax.numpy as jnp
from jax import lax
from jax.experimental import pallas as pl
from jax.experimental.pallas import tpu as pltpu
from jax.sharding import PartitionSpec as P

BLOCK = 128
ADAPTER_SCALE = 0.5
MESH = pl.DeviceIdType.MESH
F32 = jnp.float32
BF16 = jnp.bfloat16


def block_table(seg_blocks, tail_rows, page_slot, block_count, block_len):
    seg_ends = jnp.cumsum(seg_blocks, dtype=jnp.int32)
    block_ids = jnp.arange(block_count, dtype=jnp.int32)
    segment = jnp.sum(
        (block_ids[:, None] >= seg_ends[None, :]).astype(jnp.int32), axis=1, dtype=jnp.int32
    )
    one_hot = (
        segment[:, None] == jnp.arange(seg_blocks.shape[0], dtype=jnp.int32)[None, :]
    ).astype(jnp.int32)
    page_lookup = jnp.sum(one_hot * page_slot[None, :], axis=1, dtype=jnp.int32)
    last_block = jnp.sum(one_hot * seg_ends[None, :], axis=1, dtype=jnp.int32) - 1
    tail_of = jnp.sum(one_hot * tail_rows[None, :], axis=1, dtype=jnp.int32)
    active_rows = jnp.where(block_ids == last_block, tail_of, block_len)
    return (page_lookup, active_rows, one_hot)


def pick_kernel(
    tp, seg_ref, tail_ref, slot_ref, shrink, expand, s_out, e_out, oh_ref, own_ref, live_ref,
    s_buf, e_buf, s_sem, e_sem, s_out_sem, e_out_sem
):
    rep = lax.axis_index("rep")
    mine = rep * tp + lax.axis_index("tp")
    pages_here, rank, _ = shrink.shape
    segs = s_out.shape[0]
    copies = []
    for s in range(segs):
        local = slot_ref[s] - rep * pages_here
        local = jnp.minimum(jnp.maximum(local, 0), pages_here - 1)
        copies.append(
            (
                pltpu.make_async_copy(shrink.at[local], s_buf.at[s], s_sem.at[s]),
                pltpu.make_async_copy(s_buf.at[s], s_out.at[s], s_out_sem.at[s]),
            )
        )
        copies.append(
            (
                pltpu.make_async_copy(expand.at[local], e_buf.at[s], e_sem.at[s]),
                pltpu.make_async_copy(e_buf.at[s], e_out.at[s], e_out_sem.at[s]),
            )
        )
    for load, _ in copies:
        load.start()
    block = lax.broadcasted_iota(jnp.int32, oh_ref.shape, 0) + rep * tp
    group = lax.broadcasted_iota(jnp.int32, oh_ref.shape, 1) // rank
    own_group = lax.broadcasted_iota(jnp.int32, own_ref.shape, 0) // rank
    oh = jnp.zeros(oh_ref.shape, F32)
    own = jnp.zeros(own_ref.shape, F32)
    limit = jnp.int32(BLOCK)
    begin = jnp.int32(0)
    for s in range(segs):
        end = begin + seg_ref[s]
        oh = jnp.where((group == s) & (block >= begin) & (block < end), 1.0, oh)
        local = slot_ref[s] - rep * pages_here
        here = jnp.where((local >= 0) & (local < pages_here), 1.0, 0.0)
        own = jnp.where(own_group == s, here, own)
        limit = jnp.where(mine == end - 1, tail_ref[s], limit)
        begin = end
    oh_ref[...] = oh
    own_ref[...] = own
    row = lax.broadcasted_iota(jnp.int32, live_ref.shape, 0)
    live_ref[...] = jnp.where(row < limit, ADAPTER_SCALE, 0.0)
    for load, store in copies:
        load.wait()
        store.start()
    for _, store in copies:
        store.wait()


def pick_pages(tp, seg_blocks, tail_rows, page_slot, shrink_pool, expand_pool):
    segs = seg_blocks.shape[0]
    _, rank, depth = shrink_pool.shape
    width = expand_pool.shape[2]
    smem = pl.BlockSpec(memory_space=pltpu.SMEM)
    hbm = pl.BlockSpec(memory_space=pl.ANY)
    vmem = pl.BlockSpec(memory_space=pltpu.VMEM)
    return pl.pallas_call(
        functools.partial(pick_kernel, tp),
        in_specs=[smem, smem, smem, hbm, hbm],
        out_specs=[hbm, hbm, vmem, vmem, vmem],
        out_shape=[
            jax.ShapeDtypeStruct((segs, rank, depth), BF16),
            jax.ShapeDtypeStruct((segs, rank, width), BF16),
            jax.ShapeDtypeStruct((tp, segs * rank), F32),
            jax.ShapeDtypeStruct((segs * rank, 128), F32),
            jax.ShapeDtypeStruct((BLOCK, rank), F32),
        ],
        scratch_shapes=[
            pltpu.VMEM((segs, rank, depth), BF16),
            pltpu.VMEM((segs, rank, width), BF16),
        ]
        + [pltpu.SemaphoreType.DMA((segs,))] * 4,
    )(seg_blocks, tail_rows, page_slot, shrink_pool, expand_pool)


def main_kernel(
    tp, nz, tiles, nb, rank,
    hid, weight, residual, s_own, e_own, oh, own, live, out,
    hv, wbuf, ysend, yrecv, keep, rr, ll, keep_b, rr_b, ll_b, ysend_b, yrecv_b,
    acc, delta_buf, s_mine, s_recv, e_recv, page, page_in,
    rk, rk_in, res_buf, e_mine,
    hv_sem, w_sem, misc_sem, rep_send, rep_recv,
    y_send, y_recv, r_send, r_recv, l_send, l_recv,
    yb_send, yb_recv, rb_send, rb_recv, lb_send, lb_recv,
    pg_send, pg_recv, rk_send, rk_recv,
):
    t = lax.axis_index("tp")
    rep = lax.axis_index("rep")
    z = t // 2
    y = t % 2
    across = z * 2 + (1 - y)
    c = wbuf.shape[2] // 2
    half = tiles // 2
    depth = wbuf.shape[1]
    segs_rank = s_mine.shape[0]
    chunk = e_own.shape[1]
    per_chunk = chunk // c
    na = tiles - nb

    def w_copy(i):
        slot = lax.rem(i, 2)
        cols = pl.ds(pl.multiple_of(i * 2 * c, 2 * c), 2 * c)
        return pltpu.make_async_copy(weight.at[:, cols], wbuf.at[slot], w_sem.at[slot])

    def hv_copy(g):
        side = (1 - y) if g == 0 else y
        return pltpu.make_async_copy(hid.at[:, side], hv.at[g], hv_sem.at[g])

    hv_copy(0).start()
    w_copy(0).start()
    hv_copy(1).start()
    s_copy = pltpu.make_async_copy(s_own, s_mine, misc_sem.at[0])
    e_copy = pltpu.make_async_copy(e_own, e_mine, misc_sem.at[2])
    e_copy.start()
    res_copy = pltpu.make_async_copy(residual, res_buf, misc_sem.at[1])

    barrier = pltpu.get_barrier_semaphore()
    for j in range(1, tp):
        pl.semaphore_signal(
            barrier, inc=1, device_id={"tp": lax.rem(t + j, tp)}, device_id_type=MESH
        )
    pl.semaphore_signal(barrier, inc=1, device_id={"rep": 1 - rep}, device_id_type=MESH)
    pl.semaphore_wait(barrier, tp)

    e_swap = pltpu.make_async_remote_copy(
        src_ref=e_own, dst_ref=e_recv, send_sem=rep_send.at[0], recv_sem=rep_recv.at[0],
        device_id={"rep": 1 - rep}, device_id_type=MESH,
    )
    s_swap = pltpu.make_async_remote_copy(
        src_ref=s_own, dst_ref=s_recv, send_sem=rep_send.at[1], recv_sem=rep_recv.at[1],
        device_id={"rep": 1 - rep}, device_id_type=MESH,
    )
    e_swap.start()

    def y_copy(i):
        return pltpu.make_async_remote_copy(
            src_ref=ysend.at[i], dst_ref=yrecv.at[i],
            send_sem=y_send.at[i], recv_sem=y_recv.at[i],
            device_id={"tp": across}, device_id_type=MESH,
        )

    def right_copy(i, first, src):
        part = pl.ds(first, nz - first)
        return pltpu.make_async_remote_copy(
            src_ref=src.at[i, part], dst_ref=rr.at[i, part],
            send_sem=r_send.at[i], recv_sem=r_recv.at[i],
            device_id={"tp": lax.rem(t + 2, tp)}, device_id_type=MESH,
        )

    def left_copy(i, count, src):
        part = pl.ds(0, count)
        return pltpu.make_async_remote_copy(
            src_ref=src.at[i, part], dst_ref=ll.at[i, part],
            send_sem=l_send.at[i], recv_sem=l_recv.at[i],
            device_id={"tp": lax.rem(t + tp - 2, tp)}, device_id_type=MESH,
        )

    def y_copy_b(b):
        return pltpu.make_async_remote_copy(
            src_ref=ysend_b.at[b], dst_ref=yrecv_b.at[b],
            send_sem=yb_send.at[b], recv_sem=yb_recv.at[b],
            device_id={"tp": across}, device_id_type=MESH,
        )

    def right_copy_b(b, first, src):
        part = pl.ds(first, nz - first)
        return pltpu.make_async_remote_copy(
            src_ref=src.at[b, :, part], dst_ref=rr_b.at[b, :, part],
            send_sem=rb_send.at[b], recv_sem=rb_recv.at[b],
            device_id={"tp": lax.rem(t + 2, tp)}, device_id_type=MESH,
        )

    def left_copy_b(b, count, src):
        part = pl.ds(0, count)
        return pltpu.make_async_remote_copy(
            src_ref=src.at[b, :, part], dst_ref=ll_b.at[b, :, part],
            send_sem=lb_send.at[b], recv_sem=lb_recv.at[b],
            device_id={"tp": lax.rem(t + tp - 2, tp)}, device_id_type=MESH,
        )

    def product(g, w):
        value = jnp.dot(
            hv[g].reshape(nz * BLOCK, depth), w, preferred_element_type=F32
        )
        return value.astype(BF16).reshape(nz, BLOCK, 2 * c)

    def multiply_pair(i, a, b):
        slot = lax.rem(i, 2)
        w_copy(i).wait()

        @pl.when(i + 1 < half)
        def _():
            w_copy(i + 1).start()

        away = product(0, wbuf[slot])
        ysend[a] = away[:, :, :c]
        if b is None:
            ysend[a + 1] = away[:, :, c:]

            @pl.when(i == nb)
            def _():
                y_copy(a).start()
        else:
            y_copy(a).start()
            keep_b[b, 0] = away[:, :, c:]

        @pl.when(i == 0)
        def _():
            hv_copy(1).wait()

        home = product(1, wbuf[slot])
        keep[a] = home[:, :, :c]
        if b is None:
            keep[a + 1] = home[:, :, c:]
        else:
            keep_b[b, 1] = home[:, :, c:]

    def add(i, d, other):
        return (keep[i, d].astype(F32) + other[i, d].astype(F32)).astype(BF16)

    def group(g):
        @pl.when((g >= 0) & (g < na))
        def _():
            y_copy(g).wait_recv()

            @pl.when((g + 2 > nb) & (g + 2 < na))
            def _():
                y_copy(g + 2).start()

            for d in range(nz):
                keep[g, d] = add(g, d, yrecv)

        for k in range(nz):
            i = g - k

            @pl.when((z == k) & (i >= 0) & (i < na))
            def _():
                if k > 0:
                    right_copy(i, k, keep).wait_recv()
                    for d in range(k + 1, nz):
                        rr[i, d] = add(i, d, rr)
                if k < nz - 1:
                    right_copy(i, k + 1, keep if k == 0 else rr).start()

            @pl.when((z == nz - 1 - k) & (i >= 0) & (i < na))
            def _():
                me = nz - 1 - k
                if k > 0:
                    left_copy(i, me + 1, keep).wait_recv()
                    for d in range(me):
                        ll[i, d] = add(i, d, ll)
                if me > 0:
                    left_copy(i, me, keep if k == 0 else ll).start()

        i = g - (nz - 1)

        @pl.when((i >= 0) & (i < na))
        def _():
            for k in range(nz):

                @pl.when(z == k)
                def _():
                    total = keep[i, k].astype(F32)
                    if k > 0:
                        total = total + rr[i, k].astype(F32)
                    if k < nz - 1:
                        total = total + ll[i, k].astype(F32)
                    acc[jnp.where(i < nb, 2 * i, i + nb)] = total

    def add_b(b, g, d, other):
        return (keep_b[b, g, d].astype(F32) + other[b, g, d].astype(F32)).astype(BF16)

    def group_b(i):
        for k in range(nz):
            b = i - 2 * k

            @pl.when((z == k) & (b >= 0) & (b < nb))
            def _():
                if k > 0:
                    right_copy_b(b, k, keep_b).wait_recv()
                    for g in range(2):
                        for d in range(k + 1, nz):
                            rr_b[b, g, d] = add_b(b, g, d, rr_b)
                if k < nz - 1:
                    right_copy_b(b, k + 1, keep_b if k == 0 else rr_b).start()

            @pl.when((z == nz - 1 - k) & (b >= 0) & (b < nb))
            def _():
                me = nz - 1 - k
                if k > 0:
                    left_copy_b(b, me + 1, keep_b).wait_recv()
                    for g in range(2):
                        for d in range(me):
                            ll_b[b, g, d] = add_b(b, g, d, ll_b)
                if me > 0:
                    left_copy_b(b, me, keep_b if k == 0 else ll_b).start()

        b = i - 2 * (nz - 1)

        @pl.when((b >= 0) & (b < nb))
        def _():
            for k in range(nz):

                @pl.when(z == k)
                def _():
                    for g in range(2):
                        total = keep_b[b, g, k].astype(F32)
                        if k > 0:
                            total = total + rr_b[b, g, k].astype(F32)
                        if k < nz - 1:
                            total = total + ll_b[b, g, k].astype(F32)
                        if g == 0:
                            ysend_b[b] = total.astype(BF16)
                        else:
                            acc[2 * b + 1] = total

            y_copy_b(b).start()

        last = i - 2 * nz

        @pl.when((last >= 0) & (last < nb))
        def _():
            y_copy_b(last).wait_recv()
            acc[2 * last + 1] = acc[2 * last + 1] + yrecv_b[last].astype(F32)

    def page_copy(j):
        return pltpu.make_async_remote_copy(
            src_ref=page.at[lax.rem(t + j, tp)], dst_ref=page_in.at[j],
            send_sem=pg_send.at[j], recv_sem=pg_recv.at[j],
            device_id={"tp": lax.rem(t + j, tp)}, device_id_type=MESH,
        )

    def rank_copy(j):
        return pltpu.make_async_remote_copy(
            src_ref=rk.at[lax.rem(t + j, tp)], dst_ref=rk_in.at[j],
            send_sem=rk_send.at[j], recv_sem=rk_recv.at[j],
            device_id={"tp": lax.rem(t + j, tp)}, device_id_type=MESH,
        )

    def send_pages():
        e_copy.wait()
        e_swap.wait()
        row = lax.broadcasted_iota(jnp.int32, (rank, segs_rank), 0)
        col = lax.broadcasted_iota(jnp.int32, (rank, segs_rank), 1)
        diagonal = (lax.rem(col, rank) == row).astype(F32)
        is_own = jnp.concatenate([own[...].astype(BF16)] * (chunk // 128), axis=1)
        both = e_mine[...] * is_own + e_recv[...] * (1 - is_own)

        @pl.loop(0, tp)
        def _(u):
            pick = (diagonal * oh[pl.ds(u, 1), :]).astype(BF16)
            page[u] = jnp.dot(pick, both, preferred_element_type=F32).astype(BF16)

        for j in range(1, tp):
            page_copy(j).start()

    def join_shrink():
        s_copy.wait()
        s_swap.wait()
        is_own = own[...].astype(BF16)

        @pl.loop(0, depth // 128)
        def _(i):
            cols = pl.ds(pl.multiple_of(i * 128, 128), 128)
            s_mine[:, cols] = s_mine[:, cols] * is_own + s_recv[:, cols] * (1 - is_own)

    def rank_sums(g):
        half_rows = BLOCK // 2
        row = lax.rem(lax.broadcasted_iota(jnp.int32, (segs_rank, 2 * rank), 0), rank)
        col = lax.broadcasted_iota(jnp.int32, (segs_rank, 2 * rank), 1)
        top = (row == col).astype(BF16)
        low = (row + rank == col).astype(BF16)
        side = (1 - y) if g == 0 else y
        sums = lax.dot_general(
            hv[g].reshape(nz * BLOCK, depth), s_mine[...], (((1,), (1,)), ((), ())),
            preferred_element_type=F32,
        )
        for d in range(nz):
            u = 2 * d + side
            chosen = (sums[d * BLOCK : (d + 1) * BLOCK] * oh[pl.ds(u, 1), :]).astype(BF16)
            rk[u] = (
                jnp.dot(chosen[:half_rows], top, preferred_element_type=F32)
                + jnp.dot(chosen[half_rows:], low, preferred_element_type=F32)
            ).astype(BF16)

    def add_delta():
        total = rk[t].astype(F32)
        for j in range(1, tp):
            rank_copy(j).wait()
            total = total + rk_in[j].astype(F32)
        total = total.astype(BF16)
        row = lax.broadcasted_iota(jnp.int32, (2 * rank, rank), 0)
        col = lax.broadcasted_iota(jnp.int32, (2 * rank, rank), 1)
        rows = jnp.concatenate(
            [
                jnp.dot(total, (row == col).astype(BF16), preferred_element_type=F32),
                jnp.dot(total, (row == col + rank).astype(BF16), preferred_element_type=F32),
            ],
            axis=0,
        )
        rows = (rows * live[...]).astype(BF16)
        for j in range(tp):
            if j > 0:
                page_copy(j).wait()
                factor = page_in[j]
            else:
                factor = page[t]
            delta = jnp.dot(rows, factor, preferred_element_type=F32)
            owner = lax.rem(t + tp - j, tp)
            for h in range(per_chunk):
                delta_buf[owner * per_chunk + h] = delta[:, h * c : (h + 1) * c]
        res_copy.wait()
        for i in range(tiles):
            delta_buf[i] = delta_buf[i] + res_buf[:, i * c : (i + 1) * c].astype(F32)

    send_pages()
    hv_copy(0).wait()

    @pl.loop(0, half)
    def _(i):
        @pl.when(i < nb)
        def _():
            multiply_pair(i, i, i)

        @pl.when(i >= nb)
        def _():
            multiply_pair(i, 2 * i - nb, None)

        @pl.when(i == 0)
        def _():
            s_swap.start()
            s_copy.start()
            res_copy.start()

        group_b(i)
        group(i - 1)

        @pl.when(i == half - 3)
        def _():
            join_shrink()
            rank_sums(0)

        @pl.when(i == half - 2)
        def _():
            rank_sums(1)
            for j in range(1, tp):
                rank_copy(j).start()

    steps = max(na + nz, nb + 2 * nz)
    middle = (half + steps) // 2

    @pl.loop(half, middle)
    def _(i):
        group_b(i)
        group(i - 1)

    add_delta()

    @pl.loop(middle, steps)
    def _(i):
        group_b(i)
        group(i - 1)

    for i in range(tiles):
        out[:, i * c : (i + 1) * c] = (delta_buf[i] + acc[i]).astype(BF16)

    @pl.loop(0, na)
    def _(i):
        y_copy(i).wait_send()
        for k in range(nz):

            @pl.when(z == k)
            def _():
                if k < nz - 1:
                    right_copy(i, k + 1, rr).wait_send()
                if k > 0:
                    left_copy(i, k, ll).wait_send()

    @pl.loop(0, nb)
    def _(b):
        y_copy_b(b).wait_send()
        for k in range(nz):

            @pl.when(z == k)
            def _():
                if k < nz - 1:
                    right_copy_b(b, k + 1, rr_b).wait_send()
                if k > 0:
                    left_copy_b(b, k, ll_b).wait_send()


def fused(tp, rank, hidden, weight, residual, s_own, e_own, oh, own, live):
    rows, depth = hidden.shape
    width = weight.shape[1]
    nz = tp // 2
    c = min(256, e_own.shape[1])
    tiles = width // c
    segs_rank, chunk = e_own.shape
    hid = hidden.reshape(nz, 2, BLOCK, depth)
    hbm = pl.BlockSpec(memory_space=pl.ANY)
    vmem = pl.BlockSpec(memory_space=pltpu.VMEM)
    nb = (3 * tiles) // 16
    na = tiles - nb
    slab = pltpu.VMEM((na, nz, BLOCK, c), BF16)
    slab_b = pltpu.VMEM((nb, 2, nz, BLOCK, c), BF16)
    row_b = pltpu.VMEM((nb, BLOCK, c), BF16)
    dma = pltpu.SemaphoreType.DMA
    return pl.pallas_call(
        functools.partial(main_kernel, tp, nz, tiles, nb, rank),
        out_shape=jax.ShapeDtypeStruct((BLOCK, width), BF16),
        in_specs=[hbm, hbm, hbm, hbm, hbm, vmem, vmem, vmem],
        out_specs=vmem,
        scratch_shapes=[
            pltpu.VMEM((2, nz, BLOCK, depth), BF16),
            pltpu.VMEM((2, depth, 2 * c), BF16),
            slab, slab, slab, slab, slab,
            slab_b, slab_b, slab_b, row_b, row_b,
            pltpu.VMEM((tiles, BLOCK, c), F32),
            pltpu.VMEM((tiles, BLOCK, c), F32),
            pltpu.VMEM((segs_rank, depth), BF16),
            pltpu.VMEM((segs_rank, depth), BF16),
            pltpu.VMEM((segs_rank, chunk), BF16),
            pltpu.VMEM((tp, rank, chunk), BF16),
            pltpu.VMEM((tp, rank, chunk), BF16),
            pltpu.VMEM((tp, BLOCK // 2, 2 * rank), BF16),
            pltpu.VMEM((tp, BLOCK // 2, 2 * rank), BF16),
            pltpu.VMEM((BLOCK, width), BF16),
            pltpu.VMEM((segs_rank, chunk), BF16),
            dma((2,)), dma((2,)), dma((3,)), dma((2,)), dma((2,)),
            dma((na,)), dma((na,)), dma((na,)), dma((na,)), dma((na,)), dma((na,)),
            dma((nb,)), dma((nb,)), dma((nb,)), dma((nb,)), dma((nb,)), dma((nb,)),
            dma((tp,)), dma((tp,)), dma((tp,)), dma((tp,)),
        ],
        compiler_params=pltpu.CompilerParams(
            collective_id=0, has_side_effects=True, vmem_limit_bytes=60 * 1024 * 1024
        ),
        cost_estimate=pl.CostEstimate(
            flops=2 * rows * depth * (width + segs_rank),
            bytes_accessed=2 * depth * (width + rows),
            transcendentals=0,
        ),
    )(hid, weight, residual, s_own, e_own, oh, own, live)


def body_fused(hidden, residual, down_weight, shrink_pool, expand_pool, seg_blocks, tail_rows, page_slot):
    tp_count = lax.axis_size("tp")
    segs = seg_blocks.shape[0]
    _, rank, depth = shrink_pool.shape
    s_own, e_own, oh, own, live = pick_pages(
        tp_count, seg_blocks, tail_rows, page_slot, shrink_pool, expand_pool
    )
    return fused(
        tp_count, rank, hidden, down_weight, residual,
        s_own.reshape(segs * rank, depth), e_own.reshape(segs * rank, -1), oh, own, live,
    )


def body_plain(hidden, residual, down_weight, shrink_pool, expand_pool, seg_blocks, tail_rows, page_slot):
    rep_count = lax.axis_size("rep")
    rep_index = lax.axis_index("rep")
    repeated_rows = hidden.shape[0]
    blk_rep = repeated_rows // BLOCK
    every_page, every_live, _ = block_table(
        seg_blocks, tail_rows, page_slot, rep_count * blk_rep, BLOCK
    )
    page_lookup = lax.dynamic_slice_in_dim(every_page, rep_index * blk_rep, blk_rep, 0)
    active_rows = lax.dynamic_slice_in_dim(every_live, rep_index * blk_rep, blk_rep, 0)
    all_shrink = lax.all_gather(shrink_pool, "rep", axis=0, tiled=True)
    all_expand = lax.all_gather(expand_pool, "rep", axis=0, tiled=True)
    shrink_pages = jnp.take(all_shrink, page_lookup, axis=0)
    expand_pages = jnp.take(all_expand, page_lookup, axis=0)
    block_list = hidden.reshape(blk_rep, BLOCK, hidden.shape[1])
    shrink_part = jnp.einsum("bnf,bkf->bnk", block_list, shrink_pages, preferred_element_type=F32)
    rank_rows = lax.psum(shrink_part.astype(BF16), "tp")
    expanded = jnp.einsum("bnk,bkc->bnc", rank_rows, expand_pages, preferred_element_type=F32)
    mask = (jnp.arange(BLOCK, dtype=jnp.int32)[None, :] < active_rows[:, None]).astype(F32)
    delta = (ADAPTER_SCALE * expanded * mask[:, :, None]).reshape(repeated_rows, -1)
    partial = jnp.dot(hidden, down_weight, preferred_element_type=F32).astype(BF16)
    total = lax.psum_scatter(partial, "tp", scatter_dimension=0, tiled=True).astype(F32)
    total = total + lax.all_to_all(
        delta.astype(BF16), "tp", split_axis=0, concat_axis=1, tiled=True
    ).astype(F32)
    return (residual.astype(F32) + total).astype(BF16)


def body(hidden, residual, down_weight, shrink_pool, *rest):
    tp_count = lax.axis_size("tp")
    pairs = lax.axis_size("rep") == 2 and tp_count in (4, 6, 8)
    pairs = pairs and 2 * shrink_pool.shape[1] == BLOCK
    if pairs and residual.shape[0] == BLOCK and hidden.shape[0] == tp_count * BLOCK:
        return body_fused(hidden, residual, down_weight, shrink_pool, *rest)
    return body_plain(hidden, residual, down_weight, shrink_pool, *rest)


def solution(mesh):
    return jax.shard_map(
        body,
        mesh=mesh,
        in_specs=(
            P(("parts", "rep"), "tp"),
            P(("parts", "rep", "tp"), None),
            P("tp", None),
            P("rep", None, "tp"),
            P("rep", None, "tp"),
            P("parts"),
            P("parts"),
            P("parts"),
        ),
        out_specs=P(("parts", "rep", "tp"), None),
        check_vma=False,
    )
```
